256 devices in a mesh: dom: 32 (over z, y), rep: 8 (over x, core).
Axes of the slice: x: 4, y: 4, z: 8, core: 2. Of those that a mesh axis runs over, the one named last changes fastest.
Arguments:
- history_in: bfloat16 [256, 128, 1024], P('dom'), may hold values from -6 to 6
- batch_emb: bfloat16 [32768, 1024], P(('dom', 'rep')), may hold values from -6 to 6
- weight: bfloat16 [1024, 1024], P(None, 'rep'), may hold values from -0.1875 to 0.1875
- grad_fresh: bfloat16 [32768, 1024], P(('dom', 'rep')), may hold values from -6 to 6
- edge_weight: int32 [32768, 8320], P(('dom', 'rep')), may hold values from 0 to 3, as said below
- request_block: int32 [256, 32, 2], P(('dom', 'rep')), may hold values from 0 to 7
- request_count: int32 [256, 32], P(('dom', 'rep')), may hold values from 0 to 2, as said below
- batch_block: int32 [32, 8], P('dom'), may hold values from 0 to 7, as said below
Outputs:
- fresh_history: bfloat16 [256, 128, 1024], P('dom')
- weight_grad: float32 [1024, 1024], P('dom', 'rep')
- input_grad: bfloat16 [32768, 1024], P(('dom', 'rep'))
The draws below stay inside these ranges and needn't reach their ends.
Inputs may be any that keep to these rules, and one draw needn't show every extreme that they name: `request_count`: for every device, at two owners drawn from the seed the count is 2. `batch_block`: each row names every local block 0 to 7 once. `request_block`: entries of unused slots are arbitrary. `edge_weight`: most entries are zero; a row has about 4 nonzero entries in each block of 128 columns.
All inputs are finite; a program needn't handle non-finite values.
Results may differ from the reference program's by a relative error of at most 0.0056.
Values may be sent and summed in bfloat16 or wider, within the bound.
No kernel may reach another device: no remote copies, remote signals or barrier semaphores. Data moves between devices by JAX's collectives and lax.ppermute only.
A program may use at most 128 MiB of HBM per device.

```python
import math
import jax
import jax.numpy as jnp
from jax import lax

D = 1024
BLOCK = 128
CAP = 2
BB = 1
NB_OWN = 8
SLOTS = 65
ROWS = 128
ALL_ROWS = 32768
TABLE_BLOCKS = 256
N_DOM = 32
N_REP = 8


def draw_request_count(key, part):
    key = jax.random.fold_in(key, 5)
    first, second = jax.random.split(key)
    order = jax.random.permutation(first, N_DOM)
    busy = order < 2
    base = jax.random.randint(second, (N_DOM * N_REP, N_DOM), 0, CAP + 1)
    return jnp.where(busy[None, :], CAP, base).astype(jnp.int32)


def draw_batch_block(key, part):
    key = jax.random.fold_in(key, 7)
    owner_keys = jax.random.split(key, N_DOM)
    orders = jax.vmap(lambda single: jax.random.permutation(single, NB_OWN))(owner_keys)
    return orders.astype(jnp.int32)


def draw_edge_weight(key, part):
    key = jax.random.fold_in(key, 11)
    first, second = jax.random.split(key)
    shape = (ALL_ROWS, SLOTS * BLOCK)
    linked = jax.random.randint(first, shape, 0, BLOCK) < 4
    values = jax.random.randint(second, shape, 1, 4)
    drawn = jnp.where(linked, values, 0).astype(jnp.int32)
    return drawn.at[0, 0].set(3).at[0, 1].set(0)


def plant(values, key, least, high):
    longest = values.shape.index(max(values.shape))
    spots = []
    for shift in (0, 1):
        where = [jax.random.randint(jax.random.fold_in(key, axis), (), 0, length) for axis, length in enumerate(values.shape)]
        where[longest] = (where[longest] + shift) % values.shape[longest]
        spots.append(tuple(where))
    return values.at[spots[0]].set(least).at[spots[1]].set(high)


def levels(own_key, extent, cuts, smallest, largest):
    loudness, own = 1.0, jax.random.fold_in(own_key, 6)
    for axis_at, blocks in cuts:
        draws = jnp.exp(jax.random.uniform(jax.random.fold_in(own, axis_at), (blocks,), jnp.float32, smallest / len(cuts), largest / len(cuts)))
        loudness = loudness * jnp.repeat(draws, extent[axis_at] // blocks).reshape([-1 if axis == axis_at else 1 for axis in range(len(extent))])
    return loudness


def bell_draw(rng, extent, deviation, bound, pieces=(), kind=jnp.bfloat16):
    factor_of = levels(rng, extent, pieces, -0.22, 0.18) if pieces else 1.0
    values = jax.random.normal(rng, extent, jnp.float32) * deviation * factor_of
    return jnp.minimum(jnp.maximum(values, -bound), bound).astype(kind)


def setup_inputs(seed: int = 0) -> dict:
    seeds = jax.random.split(jax.random.key(seed), 9)
    history_in = bell_draw(seeds[0], (TABLE_BLOCKS, BLOCK, D), 1.0, 6.0, ((0, 32),))
    batch_emb = bell_draw(seeds[1], (ALL_ROWS, D), 1.0, 6.0, ((0, 256),))
    weight = bell_draw(seeds[2], (D, D), D ** -0.5, 0.1875, ((1, 8),))
    grad_fresh = bell_draw(seeds[3], (ALL_ROWS, D), 1.0, 6.0, ((0, 256),))
    edge_weight = draw_edge_weight(jax.random.fold_in(seeds[8], 71), 0)
    request_block = plant(jax.random.randint(seeds[5], (N_DOM * N_REP, N_DOM, CAP), 0, NB_OWN), jax.random.fold_in(seeds[5], 1), 0, NB_OWN - 1).astype(jnp.int32)
    request_count = draw_request_count(jax.random.fold_in(seeds[8], 71), 0)
    batch_block = draw_batch_block(jax.random.fold_in(seeds[8], 71), 0)
    return dict(history_in=history_in, batch_emb=batch_emb, weight=weight, grad_fresh=grad_fresh, edge_weight=edge_weight, request_block=request_block, request_count=request_count, batch_block=batch_block)


def silu_slope(value):
    sigma = jax.nn.sigmoid(value)
    return sigma * (1.0 + value * (1.0 - sigma))

def reference(history_in, batch_emb, weight, grad_fresh, edge_weight, request_block, request_count, batch_block):
    device_count = N_DOM * N_REP

    def one_device(grad_sum, device):
        rows_in = lax.dynamic_slice_in_dim(batch_emb, device * ROWS, ROWS, 0)
        cotangent = lax.dynamic_slice_in_dim(grad_fresh, device * ROWS, ROWS, 0)
        adjacency = lax.dynamic_slice_in_dim(edge_weight, device * ROWS, ROWS, 0)
        wanted = request_block[device]
        counts = request_count[device]
        flat = (jnp.arange(N_DOM, dtype=jnp.int32)[:, None] * NB_OWN + wanted).reshape(-1).astype(jnp.int32)
        halo = jnp.take(history_in, flat, axis=0).reshape(-1, D)
        valid = (jnp.arange(CAP, dtype=jnp.int32)[None, :] < counts[:, None]).reshape(-1)
        column_mask = jnp.concatenate([jnp.ones((ROWS,), jnp.float32), jnp.repeat(valid.astype(jnp.float32), BLOCK)])
        weights = adjacency.astype(jnp.float32) * column_mask[None, :]
        degree = 1.0 + lax.optimization_barrier(jnp.sum(weights, axis=1))
        scale = lax.rsqrt(degree)
        sources = jnp.concatenate([rows_in, halo], axis=0)
        summed = jnp.dot(weights.astype(jnp.bfloat16), sources, preferred_element_type=jnp.float32)
        mixed = (scale[:, None] * (rows_in.astype(jnp.float32) + summed)).astype(jnp.bfloat16)
        pre = jnp.dot(mixed, weight, preferred_element_type=jnp.float32)
        fresh = jax.nn.silu(pre).astype(jnp.bfloat16)
        gated = (cotangent.astype(jnp.float32) * silu_slope(pre)).astype(jnp.bfloat16)
        term = jnp.dot(mixed.T, gated, preferred_element_type=jnp.float32)
        back = scale[:, None] * jnp.dot(gated, weight.T, preferred_element_type=jnp.float32)
        local = weights[:, :ROWS]
        grad_rows = back + jnp.dot(local.T, back, precision=lax.Precision.HIGHEST)
        return (grad_sum + term, (fresh, grad_rows.astype(jnp.bfloat16)))
    grad_sum, outputs = lax.scan(one_device, jnp.zeros((D, D), jnp.float32), jnp.arange(device_count, dtype=jnp.int32))
    fresh_all, input_grad = outputs
    blocks = fresh_all.reshape(device_count * BB, BLOCK, D)
    positions = (jnp.arange(N_DOM, dtype=jnp.int32)[:, None] * NB_OWN + batch_block).reshape(-1).astype(jnp.int32)
    fresh_history = jnp.zeros_like(history_in).at[positions].set(blocks)
    weight_grad = grad_sum / math.sqrt(ALL_ROWS)
    return (fresh_history, weight_grad, input_grad.reshape(ALL_ROWS, D))
```

```python
import math

import jax
import jax.numpy as jnp
from jax import lax
from jax.sharding import PartitionSpec as P

Z, Y, X, CORES = 8, 4, 4, 2
BF16 = jnp.bfloat16
F32 = jnp.float32


def shift_z(value, step):
    pairs = [(z * Y + y, (z + step) % Z * Y + y) for z in range(Z) for y in range(Y)]
    return lax.ppermute(value, "dom", pairs)


def shift_y(value, step):
    pairs = [(z * Y + y, z * Y + (y + step) % Y) for z in range(Z) for y in range(Y)]
    return lax.ppermute(value, "dom", pairs)


def shift_x(value, step):
    pairs = [(x * CORES + c, (x + step) % X * CORES + c) for x in range(X) for c in range(CORES)]
    return lax.ppermute(value, "rep", pairs)


def swap_core(value):
    pairs = [(x * CORES + c, x * CORES + 1 - c) for x in range(X) for c in range(CORES)]
    return lax.ppermute(value, "rep", pairs)


def sigmoid_terms(value):
    sigma = jax.nn.sigmoid(value)
    return sigma * (1.0 + value * (1.0 - sigma))


def pick(stack, index, axis=0):
    return lax.dynamic_index_in_dim(stack, index, axis, keepdims=False)


def shards(
    history_in,
    batch_emb,
    weight,
    grad_fresh,
    edge_weight,
    request_block,
    request_count,
    batch_block,
):
    owner = lax.axis_index("dom")
    replica = lax.axis_index("rep")
    z, y = owner // Y, owner % Y
    x, core = replica // CORES, replica % CORES
    blocks, block, width = history_in.shape
    rows = batch_emb.shape[0]
    half = width // CORES

    table = lax.dynamic_slice(history_in, (0, 0, core * half), (blocks, block, half))
    table = table.reshape(blocks * block, half)
    up, down = [shift_z(table, 1)], [shift_z(table, -1)]

    count = request_count[0].reshape(Z, Y, 1)
    wanted = request_block[0].reshape(Z, Y, 2)
    valid = jnp.arange(2, dtype=jnp.int32)[None, None, :] < count
    code = jnp.where(valid, wanted, -1)
    lanes = jnp.repeat(code.reshape(Z, Y, 2, 1), block, axis=3).reshape(Z, Y, 2 * block)
    edges = edge_weight[:, rows:].reshape(rows, Z, Y, 2 * block)
    masked = jnp.where((lanes >= 0)[None], edges, 0)
    degree = 1.0 + (
        jnp.sum(edge_weight[:, :rows].astype(F32), axis=1)
        + jnp.sum(masked.astype(F32), axis=(1, 2, 3))
    )
    scale = lax.rsqrt(degree)
    message = jnp.concatenate(
        [
            edges.astype(BF16).transpose(2, 1, 0, 3),
            jnp.broadcast_to(
                lanes.astype(BF16).transpose(1, 0, 2)[:, :, None, :], (Y, Z, 16, 2 * block)
            ),
        ],
        axis=2,
    )
    near = [pick(message, y)] + [
        shift_y(pick(message, (y + step) % Y), step) for step in range(1, Y)
    ]
    here = jnp.stack(near)
    asked = jnp.stack([here, swap_core(here)])

    def merged(at):
        part = pick(asked, at, axis=2)
        part = part.reshape(CORES * Y, part.shape[2], 2, block)
        names = part[:, rows]
        body = part[:, :rows]
        choice = jnp.arange(blocks, dtype=jnp.int32).astype(BF16)
        hit = (names[:, :, None, :] == choice[None, None, :, None]).astype(BF16)
        both = body[:, :, :, None, :] * hit[:, None]
        return (both[:, :, 0] + both[:, :, 1]).reshape(CORES * Y * rows, blocks * block)

    def served(at, piece):
        return jnp.dot(merged(at % Z), piece, preferred_element_type=F32)

    total = served(z, table)
    for step in range(1, 4):
        if step > 1:
            up.append(shift_z(up[-1], 1))
            down.append(shift_z(down[-1], -1))
        total = total + served(z - step + Z, up[step - 1])
        total = total + served(z + step, down[step - 1])
    middle = blocks * block // 2
    far = jnp.concatenate([shift_z(up[2][:middle], 1), shift_z(down[2][middle:], -1)])
    total = total + served(z + 4, far)

    total = total.reshape(CORES, Y, rows, half)
    other = swap_core(total[1].astype(BF16)).astype(F32)
    mine = total[0]
    sums = jnp.where(
        core == 0,
        jnp.concatenate([mine, other], axis=2),
        jnp.concatenate([other, mine], axis=2),
    )
    arrived = [shift_y(sums[step].astype(BF16), -step).astype(F32) for step in range(1, Y)]
    local = edge_weight[:, :rows].astype(F32)
    own = batch_emb.astype(F32) + jnp.dot(
        local.astype(BF16), batch_emb, preferred_element_type=F32
    )
    mixed = (scale[:, None] * (own + sums[0] + arrived[0] + arrived[1] + arrived[2])).astype(BF16)

    full_weight = lax.all_gather(weight, "rep", axis=1, tiled=True)
    left, right = shift_x(mixed, 1), shift_x(mixed, -1)
    low, high = shift_x(left[: rows // 2], 1), shift_x(right[rows // 2 :], -1)
    column = jnp.concatenate([mixed, left, right, low, high])
    every = jnp.concatenate([column, swap_core(column)])
    offsets = jnp.array([0, X - 1, 1, 2], jnp.int32)
    places = ((x + offsets) % X)[None, :] * CORES + jnp.stack([core, 1 - core])[:, None]
    places = places.reshape(-1)

    grads = lax.all_to_all(grad_fresh, "rep", split_axis=1, concat_axis=0, tiled=True)
    grads = jnp.take(grads.reshape(X * CORES, rows, -1), places, axis=0)
    grads = grads.reshape(X * CORES * rows, -1)
    pre_columns = jnp.dot(every, weight, preferred_element_type=F32)
    gated_columns = (grads.astype(F32) * sigmoid_terms(pre_columns)).astype(BF16)
    term = lax.dot_general(
        every, gated_columns, (((0,), (0,)), ((), ())), preferred_element_type=F32
    )
    terms = lax.all_to_all(term, "dom", split_axis=0, concat_axis=0, tiled=True)
    total_rows = rows * Z * Y * X * CORES
    weight_grad = jnp.sum(terms.reshape(Z * Y, -1, term.shape[1]), axis=0) / math.sqrt(total_rows)

    targets = jnp.take(batch_block[0], places)
    order = jnp.argmax(
        targets[None, :] == jnp.arange(blocks, dtype=jnp.int32)[:, None], axis=1
    )
    ordered = jnp.take(every.reshape(X * CORES, rows, width), order, axis=0)
    pre_all = jnp.dot(ordered.reshape(-1, width), full_weight, preferred_element_type=F32)
    fresh_history = jax.nn.silu(pre_all).astype(BF16).reshape(blocks, block, width)

    pre = jnp.dot(mixed, full_weight, preferred_element_type=F32)
    gated = (grad_fresh.astype(F32) * sigmoid_terms(pre)).astype(BF16)
    backward = lax.dot_general(
        gated, full_weight, (((1,), (1,)), ((), ())), preferred_element_type=F32
    )
    back = scale[:, None] * backward
    grad_rows = back + jnp.dot(local.T, back, precision=lax.Precision.HIGHEST)
    return (fresh_history, weight_grad, grad_rows.astype(BF16))


def solution(mesh):
    placed = (
        P("dom", None, None),
        P(("dom", "rep"), None),
        P(None, "rep"),
        P(("dom", "rep"), None),
        P(("dom", "rep"), None),
        P(("dom", "rep"), None, None),
        P(("dom", "rep"), None),
        P("dom", None),
    )
    return jax.shard_map(
        shards,
        mesh=mesh,
        in_specs=placed,
        out_specs=(P("dom", None, None), P("dom", "rep"), P(("dom", "rep"), None)),
        check_vma=False,
    )
```

```python
import functools
import math

import jax
import jax.numpy as jnp
from jax import lax
from jax.experimental import pallas as pl
from jax.experimental.pallas import tpu as pltpu
from jax.sharding import PartitionSpec as P

Z, Y, X, CORES = 8, 4, 4, 2
CAP = 2
BLOCK = 128
NAMES = 16
BF16 = jnp.bfloat16
F32 = jnp.float32
VMEM = pl.BlockSpec(memory_space=pltpu.VMEM)
SMEM = pl.BlockSpec(memory_space=pltpu.SMEM)
LIMIT = 50 * 2**20


def shift_z(value, step):
    pairs = [(z * Y + y, (z + step) % Z * Y + y) for z in range(Z) for y in range(Y)]
    return lax.ppermute(value, "dom", pairs)


def shift_y(value, step):
    pairs = [(z * Y + y, z * Y + (y + step) % Y) for z in range(Z) for y in range(Y)]
    return lax.ppermute(value, "dom", pairs)


def shift_x(value, step):
    pairs = [(x * CORES + c, (x + step) % X * CORES + c) for x in range(X) for c in range(CORES)]
    return lax.ppermute(value, "rep", pairs)


def swap_core(value):
    pairs = [(x * CORES + c, x * CORES + 1 - c) for x in range(X) for c in range(CORES)]
    return lax.ppermute(value, "rep", pairs)


def slope(value):
    sigma = 1.0 / (1.0 + jnp.exp(-value))
    return sigma * (1.0 + value * (1.0 - sigma))


def params():
    return pltpu.CompilerParams(vmem_limit_bytes=LIMIT)


def cost(flops, moved):
    return pl.CostEstimate(flops=flops, bytes_accessed=moved, transcendentals=0)


def pack_kernel(at_ref, edge_ref, code_ref, batch_ref, *outs):
    near, (keep_ref, give_ref, local_ref, scale_ref) = outs[:Y], outs[Y:]
    y, core = at_ref[0], at_ref[1]
    rows, width = batch_ref.shape
    half = width // CORES
    pair = CAP * BLOCK
    sums = jnp.zeros((rows, pair), jnp.int32)
    for step in range(Y):
        column = lax.rem(y + step, Y)
        for z in range(Z):
            slot = z * Y + column
            edges = edge_ref[:, pl.ds(pl.multiple_of(rows + slot * pair, BLOCK), pair)]
            code = code_ref[pl.ds(slot, 1), :]
            near[step][z, :rows, :] = edges.astype(F32).astype(BF16)
            near[step][z, rows:, :] = jnp.broadcast_to(code, (NAMES, pair)).astype(F32).astype(BF16)
            sums = sums + jnp.where(code >= 0, edges, 0)
    local = edge_ref[:, :rows].astype(F32)
    degree = (
        1.0
        + jnp.sum(local, axis=1, keepdims=True)
        + jnp.sum(sums.astype(F32), axis=1, keepdims=True)
    )
    scale = jnp.broadcast_to(lax.rsqrt(degree), (rows, BLOCK))
    scale_ref[...] = scale
    local_ref[...] = local.astype(BF16)
    for ref, part in ((keep_ref, core), (give_ref, 1 - core)):
        batch = batch_ref[:, pl.ds(pl.multiple_of(part * half, BLOCK), half)]
        ref[:, :half] = batch.astype(F32) + jnp.dot(
            local.astype(BF16), batch, preferred_element_type=F32
        )
        ref[:, half:] = scale


def pack(at, edge_weight, code, batch_emb):
    rows, width = batch_emb.shape
    half = width // CORES
    message = jax.ShapeDtypeStruct((Z, rows + NAMES, CAP * BLOCK), BF16)
    own = jax.ShapeDtypeStruct((rows, half + BLOCK), F32)
    return pl.pallas_call(
        pack_kernel,
        out_shape=[message] * Y
        + [
            own,
            own,
            jax.ShapeDtypeStruct((rows, rows), BF16),
            jax.ShapeDtypeStruct((rows, BLOCK), F32),
        ],
        in_specs=[SMEM, VMEM, VMEM, VMEM],
        out_specs=[VMEM] * (Y + 4),
        compiler_params=params(),
        cost_estimate=cost(2 * rows * rows * width, 8 * 2**20),
        name="pack",
    )(at, edge_weight, code, batch_emb)


def split_kernel(first_ref, second_ref, low_ref, high_ref):
    low_ref[...] = first_ref[...]
    high_ref[...] = second_ref[...]


def split(first, second, rows):
    tile = BLOCK
    steps = rows // tile
    part = jax.ShapeDtypeStruct((rows, first.shape[1]), first.dtype)
    spec = pl.BlockSpec((tile, first.shape[1]), lambda i: (i, 0))
    return pl.pallas_call(
        split_kernel,
        grid=(steps,),
        out_shape=[part, part],
        in_specs=[spec, pl.BlockSpec((tile, first.shape[1]), lambda i: (i + steps, 0))],
        out_specs=[spec, spec],
        compiler_params=params(),
        cost_estimate=cost(0, 4 * rows * first.shape[1] * 2),
        name="split",
    )(first, second)


def serve_kernel(owners, pieces, first, last, at_ref, *refs):
    senders = CORES * Y
    count = owners * senders
    messages, refs = refs[:count], refs[count:]
    tables, refs = refs[: sum(pieces)], refs[sum(pieces) :]
    if not first:
        total_ref, refs = refs[0], refs[1:]
    outs, merged = refs[:-1], refs[-1]
    depth = merged.shape[1] // owners
    blocks = depth // BLOCK

    @pl.when(pl.program_id(0) == 0)
    def _():
        for owner in range(owners):
            for sender in range(senders):
                ref = messages[owner * senders + sender]
                names = ref[0, BLOCK:, :].astype(F32)
                body = ref[0, :BLOCK, :].reshape(BLOCK // NAMES, NAMES, CAP * BLOCK)
                for block in range(blocks):
                    hit = jnp.where(names == float(block), 1.0, 0.0).astype(BF16)
                    part = body * hit[None]
                    both = part[:, :, :BLOCK] + part[:, :, BLOCK:]
                    merged[
                        sender * BLOCK : (sender + 1) * BLOCK,
                        owner * depth + block * BLOCK : owner * depth + (block + 1) * BLOCK,
                    ] = both.reshape(BLOCK, BLOCK)

    for step in range(Y):
        products = []
        for core in range(CORES):
            sender = core * Y + step
            rows = slice(sender * BLOCK, (sender + 1) * BLOCK)
            value = None if first else total_ref[core, step]
            start = 0
            for table in tables:
                product = jnp.dot(
                    merged[rows, start : start + table.shape[0]],
                    table[...],
                    preferred_element_type=F32,
                )
                value = product if value is None else value + product
                start += table.shape[0]
            products.append(value)
        for core in range(CORES):
            if last:
                outs[step][core] = products[core].astype(outs[step].dtype)
            else:
                outs[0][core, step] = products[core]


def serve(at, messages, tables, total=None, last=False, chunk=256):
    owners = len(tables)
    depth = sum(piece.shape[0] for piece in tables[0])
    half = tables[0][0].shape[1]
    flat = [piece for pieces in tables for piece in pieces]
    rows = messages[0].shape[1]

    def message_spec(owner):
        return pl.BlockSpec((1, rows, CAP * BLOCK), lambda j, at_ref: (at_ref[owner], 0, 0))

    in_specs = [message_spec(owner) for owner in range(owners) for _ in messages]
    in_specs += [pl.BlockSpec((piece.shape[0], chunk), lambda j, at_ref: (0, j)) for piece in flat]
    total_spec = pl.BlockSpec((CORES, Y, BLOCK, chunk), lambda j, at_ref: (0, 0, 0, j))
    args = list(messages) * owners + flat
    if total is not None:
        in_specs.append(total_spec)
        args.append(total)
    if last:
        out_shape = [
            jax.ShapeDtypeStruct((CORES, BLOCK, half), F32 if step == 0 else BF16)
            for step in range(Y)
        ]
        out_specs = [
            pl.BlockSpec((CORES, BLOCK, chunk), lambda j, at_ref: (0, 0, j)) for _ in range(Y)
        ]
    else:
        out_shape = [jax.ShapeDtypeStruct((CORES, Y, BLOCK, half), F32)]
        out_specs = [total_spec]
    kernel = functools.partial(
        serve_kernel, owners, [len(pieces) for pieces in tables], total is None, last
    )
    senders = CORES * Y * BLOCK
    result = pl.pallas_call(
        kernel,
        grid_spec=pltpu.PrefetchScalarGridSpec(
            num_scalar_prefetch=1,
            grid=(half // chunk,),
            in_specs=in_specs,
            out_specs=out_specs,
            scratch_shapes=[pltpu.VMEM((senders, owners * depth), BF16)],
        ),
        out_shape=out_shape,
        compiler_params=params(),
        cost_estimate=cost(2 * senders * owners * depth * half, owners * 2 * 2**20),
        name="serve",
    )(at, *args)
    return result if last else result[0]


def mix_kernel(keep_ref, peer_ref, own_ref, *refs):
    arrived, out_ref = refs[:-1], refs[-1]
    half = own_ref.shape[2]
    for core, ref in enumerate((keep_ref, peer_ref)):
        value = ref[:, :half] + own_ref[core]
        for part in arrived:
            value = value + part[core].astype(F32)
        scale = ref[:, half : half + 1]
        out_ref[core] = (scale * value).astype(BF16)


def mix(keep, peer, own, arrived):
    return pl.pallas_call(
        mix_kernel,
        out_shape=jax.ShapeDtypeStruct(own.shape, BF16),
        in_specs=[VMEM] * (3 + len(arrived)),
        out_specs=VMEM,
        compiler_params=params(),
        cost_estimate=cost(2**20, 2 * 2**20),
        name="mix",
    )(keep, peer, own, *arrived)


def halves(at_ref, ref):
    core = at_ref[1]
    half = ref.shape[0] // CORES
    mine = ref[pl.ds(pl.multiple_of(core * half, BLOCK), half), :]
    other = ref[pl.ds(pl.multiple_of((1 - core) * half, BLOCK), half), :]
    return mine, other


def row_pair(mine_ref, other_ref):
    shape = (CORES * BLOCK, mine_ref.shape[2])
    mine = mine_ref[...].reshape(shape)
    other = jnp.concatenate([other_ref[1], other_ref[0]], axis=0)
    return mine, other


def term_kernel(at_ref, weight_ref, grads_ref, *refs):
    mixed, outs, whole_ref = refs[: 2 * X], refs[2 * X : -1], refs[-1]
    core = at_ref[1]
    weight_mine, weight_other = halves(at_ref, weight_ref)
    half = weight_mine.shape[0]
    sums = [None, None]
    for step in range(X):
        rows = row_pair(mixed[2 * step], mixed[2 * step + 1])
        pre = jnp.dot(rows[0], weight_mine, preferred_element_type=F32) + jnp.dot(
            rows[1], weight_other, preferred_element_type=F32
        )
        grads = jnp.concatenate(
            [grads_ref[at_ref[2 + 2 * step + part]] for part in range(CORES)], axis=0
        )
        gated = (grads.astype(F32) * slope(pre)).T.astype(BF16)
        for part in range(CORES):
            product = jnp.dot(gated, rows[part], preferred_element_type=F32)
            sums[part] = product if sums[part] is None else sums[part] + product
    height = half // (Z * Y // CORES)
    whole_ref[pl.ds(pl.multiple_of(core * half, BLOCK), half), :] = sums[0].T
    whole_ref[pl.ds(pl.multiple_of((1 - core) * half, BLOCK), half), :] = sums[1].T
    for step, out_ref in enumerate(outs):
        column = lax.rem(at_ref[0] - step + Y, Y)
        for z in range(Z):
            start = pl.multiple_of((z * Y + column) * height, height)
            out_ref[z * height : (z + 1) * height, :] = whole_ref[pl.ds(start, height), :]


def weight_term(at, weight, grads, mixed):
    return pl.pallas_call(
        term_kernel,
        out_shape=[jax.ShapeDtypeStruct((weight.shape[0] // Y, weight.shape[1]), F32)] * Y,
        in_specs=[SMEM] + [VMEM] * (2 + len(mixed)),
        out_specs=[VMEM] * Y,
        scratch_shapes=[pltpu.VMEM(weight.shape, F32)],
        compiler_params=params(),
        cost_estimate=cost(2**29, 3 * 2**20),
        name="term",
    )(at, weight, grads, *mixed)


def fresh_kernel(at_ref, weight_ref, *refs):
    mixed, out_ref = refs[:-1], refs[-1]
    weight_mine, weight_other = halves(at_ref, weight_ref)
    for step in range(X):
        rows = row_pair(mixed[2 * step], mixed[2 * step + 1])
        pre = jnp.dot(rows[0], weight_mine, preferred_element_type=F32) + jnp.dot(
            rows[1], weight_other, preferred_element_type=F32
        )
        value = (pre / (1.0 + jnp.exp(-pre))).astype(BF16)
        for part in range(CORES):
            place = at_ref[2 + X * CORES + 2 * step + part]
            out_ref[place] = value[part * BLOCK : (part + 1) * BLOCK]


def fresh_blocks(at, weight, mixed):
    width = weight.shape[0]
    return pl.pallas_call(
        fresh_kernel,
        out_shape=jax.ShapeDtypeStruct((X * CORES, BLOCK, width), BF16),
        in_specs=[SMEM] + [VMEM] * (1 + len(mixed)),
        out_specs=VMEM,
        compiler_params=params(),
        cost_estimate=cost(2**31, 6 * 2**20),
        name="fresh",
    )(at, weight, *mixed)


def back_kernel(at_ref, weight_ref, mine_ref, other_ref, grad_ref, scale_ref, local_ref, out_ref):
    weight_mine, weight_other = halves(at_ref, weight_ref)
    pre = jnp.dot(mine_ref[0], weight_mine, preferred_element_type=F32) + jnp.dot(
        other_ref[1], weight_other, preferred_element_type=F32
    )
    gated = (grad_ref[...].astype(F32) * slope(pre)).astype(BF16)
    back = scale_ref[:, :1] * lax.dot_general(
        gated, weight_ref[...], (((1,), (1,)), ((), ())), preferred_element_type=F32
    )
    local = local_ref[...].astype(F32).T.astype(BF16)
    value, rest = back, back
    for _ in range(3):
        part = rest.astype(BF16)
        value = value + jnp.dot(local, part, preferred_element_type=F32)
        rest = rest - part.astype(F32)
    out_ref[...] = value.astype(BF16)


def input_rows(at, weight, mine, other, grad_fresh, scale, local):
    return pl.pallas_call(
        back_kernel,
        out_shape=jax.ShapeDtypeStruct(grad_fresh.shape, BF16),
        in_specs=[SMEM] + [VMEM] * 6,
        out_specs=VMEM,
        compiler_params=params(),
        cost_estimate=cost(2**29 + 2**28, 4 * 2**20),
        name="back",
    )(at, weight, mine, other, grad_fresh, scale, local)


def shards(
    history_in,
    batch_emb,
    weight,
    grad_fresh,
    edge_weight,
    request_block,
    request_count,
    batch_block,
):
    owner = lax.axis_index("dom")
    replica = lax.axis_index("rep")
    z, y = owner // Y, owner % Y
    x, core = replica // CORES, replica % CORES
    blocks, block, width = history_in.shape
    rows = batch_emb.shape[0]
    half = width // CORES

    table = lax.dynamic_slice(history_in, (0, 0, core * half), (blocks, block, half))
    table = table.reshape(blocks * block, half)
    up, down = [table, shift_z(table, 1)], [table, shift_z(table, -1)]

    offsets = jnp.array([0, X - 1, 1, 2], jnp.int32)
    places = ((x + offsets) % X)[:, None] * CORES + jnp.stack([core, 1 - core])[None, :]
    places = places.reshape(-1)
    targets = jnp.take(batch_block[0], places)
    at = jnp.concatenate([jnp.stack([y, core]), places, targets]).astype(jnp.int32)

    valid = jnp.arange(CAP, dtype=jnp.int32)[None, :] < request_count[0][:, None]
    code = jnp.where(valid, request_block[0], -1)
    code = jnp.repeat(code, block, axis=1)
    *near, keep, give, local, scale = pack(at, edge_weight, code, batch_emb)
    peer = swap_core(give)
    here = [near[0]] + [shift_y(near[step], step) for step in range(1, Y)]

    full_weight = lax.all_gather(weight, "rep", axis=1, tiled=True)
    grads = lax.all_to_all(grad_fresh, "rep", split_axis=1, concat_axis=0, tiled=True)
    grads = grads.reshape(X * CORES, rows, -1)

    def owners_at(*steps):
        return jnp.stack([(z + step) % Z for step in steps]).astype(jnp.int32)

    up[1], down[1], here[1], here[3] = lax.optimization_barrier(
        (up[1], down[1], here[1], here[3])
    )
    up.append(shift_z(up[1], 1))
    down.append(shift_z(down[1], -1))
    up[2], down[2], here[2], grads, peer = lax.optimization_barrier(
        (up[2], down[2], here[2], grads, peer)
    )
    up.append(shift_z(up[2], 1))
    down.append(shift_z(down[2], -1))
    messages = here + [swap_core(message) for message in here]
    total = serve(owners_at(0, 7, 1), messages, [[table], [up[1]], [down[1]]])
    total = serve(owners_at(6, 2), messages, [[up[2]], [down[2]]], total)
    up[3], down[3], total = lax.optimization_barrier((up[3], down[3], total))
    middle = blocks * block // 2
    low, high = split(up[3], down[3], middle)
    far = [shift_z(low, 1), shift_z(high, -1)]
    total = serve(owners_at(5, 3), messages, [[up[3]], [down[3]]], total)
    sums = serve(owners_at(4), messages, [far], total, last=True)

    arrived = [shift_y(sums[step], -step) for step in range(1, Y)]
    mixed = [mix(keep, peer, sums[0], arrived)]
    mixed += [shift_x(mixed[0], 1), shift_x(mixed[0], -1), shift_x(mixed[0], 2)]
    own_other = swap_core(mixed[0])
    input_grad = input_rows(at, full_weight, mixed[0], own_other, grad_fresh, scale, local)
    mixed[3], input_grad = lax.optimization_barrier((mixed[3], input_grad))
    mixed = [mixed[0], own_other] + [
        part for mine in mixed[1:] for part in (mine, swap_core(mine))
    ]
    columns = [[z * Y + column for z in range(Z)] for column in range(Y)]
    terms = weight_term(at, weight, grads, mixed)
    others = [shift_y(terms[step], -step) for step in range(1, Y)]
    fresh_history = fresh_blocks(at, full_weight, mixed)
    others, fresh_history = lax.optimization_barrier((others, fresh_history))
    part = terms[0] + others[0] + others[1] + others[2]
    part = lax.all_to_all(
        part, "dom", split_axis=0, concat_axis=0, tiled=True, axis_index_groups=columns
    )
    total_rows = rows * Z * Y * X * CORES
    weight_grad = jnp.sum(part.reshape(Z, -1, weight.shape[1]), axis=0) / math.sqrt(total_rows)
    return (fresh_history, weight_grad, input_grad)


def solution(mesh):
    placed = (
        P("dom", None, None),
        P(("dom", "rep"), None),
        P(None, "rep"),
        P(("dom", "rep"), None),
        P(("dom", "rep"), None),
        P(("dom", "rep"), None, None),
        P(("dom", "rep"), None),
        P("dom", None),
    )
    return jax.shard_map(
        shards,
        mesh=mesh,
        in_specs=placed,
        out_specs=(P("dom", None, None), P("dom", "rep"), P(("dom", "rep"), None)),
        check_vma=False,
    )
```

```python
import functools
import math

import jax
import jax.numpy as jnp
from jax import lax
from jax.experimental import pallas as pl
from jax.experimental.pallas import tpu as pltpu
from jax.sharding import PartitionSpec as P

Z, Y, X, CORES = 8, 4, 4, 2
CAP = 2
KNOWN = 4
BLOCK = 128
NAMES = 16
BF16 = jnp.bfloat16
F32 = jnp.float32
VMEM = pl.BlockSpec(memory_space=pltpu.VMEM)
SMEM = pl.BlockSpec(memory_space=pltpu.SMEM)
LIMIT = 48 * 2**20
WHOLE = 60 * 2**20


def shift_z(value, step):
    pairs = [(z * Y + y, (z + step) % Z * Y + y) for z in range(Z) for y in range(Y)]
    return lax.ppermute(value, "dom", pairs)


def shift_y(value, step):
    pairs = [(z * Y + y, z * Y + (y + step) % Y) for z in range(Z) for y in range(Y)]
    return lax.ppermute(value, "dom", pairs)


def shift_x(value, step):
    pairs = [(x * CORES + c, (x + step) % X * CORES + c) for x in range(X) for c in range(CORES)]
    return lax.ppermute(value, "rep", pairs)


def swap_even(value):
    pairs = [(x * CORES + c, (x ^ 1) * CORES + c) for x in range(X) for c in range(CORES)]
    return lax.ppermute(value, "rep", pairs)


def swap_odd(value):
    pairs = [
        (x * CORES + c, (x - 1 + 2 * (x % 2)) % X * CORES + c) for x in range(X) for c in range(CORES)
    ]
    return lax.ppermute(value, "rep", pairs)


def swap_core(value):
    pairs = [(x * CORES + c, x * CORES + 1 - c) for x in range(X) for c in range(CORES)]
    return lax.ppermute(value, "rep", pairs)


def slope(value):
    sigma = 1.0 / (1.0 + jnp.exp(-value))
    return sigma * (1.0 + value * (1.0 - sigma))


def params(limit=LIMIT):
    return pltpu.CompilerParams(vmem_limit_bytes=limit)


def cost(flops, moved):
    return pl.CostEstimate(flops=flops, bytes_accessed=moved, transcendentals=0)


def pack_kernel(at_ref, edge_ref, code_ref, batch_ref, *outs):
    near, (keep_ref, give_ref, local_ref, scale_ref) = outs[:Y], outs[Y:]
    y, core = at_ref[0], at_ref[1]
    rows, width = batch_ref.shape
    half = width // CORES
    pair = CAP * BLOCK
    sums = jnp.zeros((rows, pair), jnp.int32)
    for step in range(Y):
        column = lax.rem(y + step, Y)
        for z in range(Z):
            slot = z * Y + column
            edges = edge_ref[:, pl.ds(pl.multiple_of(rows + slot * pair, BLOCK), pair)]
            code = code_ref[pl.ds(slot, 1), :]
            near[step][z, :rows, :] = edges.astype(F32).astype(BF16)
            near[step][z, rows:, :] = jnp.broadcast_to(code, (NAMES, pair)).astype(F32).astype(BF16)
            sums = sums + jnp.where(code >= 0, edges, 0)
    local = edge_ref[:, :rows].astype(F32)
    degree = (
        1.0
        + jnp.sum(local, axis=1, keepdims=True)
        + jnp.sum(sums.astype(F32), axis=1, keepdims=True)
    )
    scale = jnp.broadcast_to(lax.rsqrt(degree), (rows, BLOCK))
    scale_ref[...] = scale
    local_ref[...] = local.astype(BF16)
    for ref, part in ((keep_ref, core), (give_ref, 1 - core)):
        batch = batch_ref[:, pl.ds(pl.multiple_of(part * half, BLOCK), half)]
        ref[:, :half] = batch.astype(F32) + jnp.dot(
            local.astype(BF16), batch, preferred_element_type=F32
        )
        ref[:, half:] = scale


def pack(at, edge_weight, code, batch_emb):
    rows, width = batch_emb.shape
    half = width // CORES
    message = jax.ShapeDtypeStruct((Z, rows + NAMES, CAP * BLOCK), BF16)
    own = jax.ShapeDtypeStruct((rows, half + BLOCK), F32)
    return pl.pallas_call(
        pack_kernel,
        out_shape=[message] * Y
        + [
            own,
            own,
            jax.ShapeDtypeStruct((rows, rows), BF16),
            jax.ShapeDtypeStruct((rows, BLOCK), F32),
        ],
        in_specs=[SMEM, VMEM, VMEM, VMEM],
        out_specs=[VMEM] * (Y + 4),
        compiler_params=params(WHOLE),
        cost_estimate=cost(2 * rows * rows * width, 8 * 2**20),
        name="pack",
    )(at, edge_weight, code, batch_emb)


def serve_kernel(owners, parts, own, group, first, last, at_ref, *refs):
    each = Y + 1
    messages, refs = refs[: owners * each], refs[owners * each :]
    pieces, refs = refs[: sum(parts)], refs[sum(parts) :]
    if not first:
        total_ref, refs = refs[0], refs[1:]
    outs, (merged, tables) = refs[:-2], refs[-2:]
    depth = tables.shape[0] // owners

    @pl.when(pl.program_id(0) == 0)
    def _():
        row = 0
        for piece in pieces:
            value = piece[...].reshape(-1, piece.shape[-1])
            tables[row : row + value.shape[0], :] = value
            row += value.shape[0]

    for step in range(Y):

        @pl.when(pl.program_id(0) == step // group)
        def _(step=step):
            place_in = step % group
            top = place_in * CORES * BLOCK
            for owner in range(owners):
                for core in range(CORES):
                    ref = messages[owner * each + (Y if core else step)]
                    ref = ref.at[step, 0] if core else ref.at[0]
                    names = ref[BLOCK:, :].astype(F32)
                    body = ref[:BLOCK, :].reshape(BLOCK // NAMES, NAMES, CAP * BLOCK)
                    for place in range(depth // BLOCK):
                        block = float(place)
                        if not (own and owner == 0):
                            part, rest = divmod(place, depth // BLOCK // 2)
                            block = (at_ref[1 + part] + rest).astype(F32)
                        hit = jnp.where(names == block, 1.0, 0.0).astype(BF16)
                        part = body * hit[None]
                        both = part[:, :, :BLOCK] + part[:, :, BLOCK:]
                        column = owner * depth + place * BLOCK
                        row = top + core * BLOCK
                        merged[row : row + BLOCK, column : column + BLOCK] = both.reshape(
                            BLOCK, BLOCK
                        )
            value = jnp.dot(
                merged[top : top + CORES * BLOCK, :], tables[...], preferred_element_type=F32
            )
            value = value.reshape(CORES, BLOCK, value.shape[1])
            if not first:
                value = total_ref[:, place_in] + value
            if last:
                outs[step][...] = value.astype(outs[step].dtype)
            else:
                outs[0][:, place_in] = value


def serve(at, here, there, tables, half, depth, total=None, last=False, own=False):
    owners = len(tables)
    group = Y if last else 2
    flat = [piece for pieces in tables for piece in pieces]

    def message_spec(owner):
        shape = (1,) + here[0].shape[1:]
        return pl.BlockSpec(shape, lambda i, at_ref: (at_ref[KNOWN + owner], 0, 0))

    def other_spec(owner):
        shape = (Y, 1) + here[0].shape[1:]
        return pl.BlockSpec(shape, lambda i, at_ref: (0, at_ref[KNOWN + owner], 0, 0))

    def piece_spec(piece):
        if piece.ndim == 3:
            shape = piece.shape[:2] + (half,)
            return pl.BlockSpec(shape, lambda i, at_ref: (0, 0, at_ref[KNOWN - 1]))
        return pl.BlockSpec(piece.shape, lambda i, at_ref: (0, 0))

    in_specs = []
    for owner in range(owners):
        in_specs += [message_spec(owner)] * Y + [other_spec(owner)]
    in_specs += [piece_spec(piece) for piece in flat]
    total_spec = pl.BlockSpec((CORES, group, BLOCK, half), lambda i, at_ref: (0, i, 0, 0))
    args = (list(here) + [there]) * owners + flat
    if total is not None:
        in_specs.append(total_spec)
        args.append(total)
    if last:
        out_shape = [
            jax.ShapeDtypeStruct((CORES, BLOCK, half), F32 if step == 0 else BF16)
            for step in range(Y)
        ]
        out_specs = [pl.BlockSpec((CORES, BLOCK, half), lambda i, at_ref: (0, 0, 0))] * Y
    else:
        out_shape = [jax.ShapeDtypeStruct((CORES, Y, BLOCK, half), F32)]
        out_specs = [total_spec]
    result = pl.pallas_call(
        functools.partial(
            serve_kernel,
            owners,
            [len(pieces) for pieces in tables],
            own,
            group,
            total is None,
            last,
        ),
        grid_spec=pltpu.PrefetchScalarGridSpec(
            num_scalar_prefetch=1,
            grid=(Y // group,),
            in_specs=in_specs,
            out_specs=out_specs,
            scratch_shapes=[
                pltpu.VMEM((group * CORES * BLOCK, owners * depth), BF16),
                pltpu.VMEM((owners * depth, half), BF16),
            ],
        ),
        out_shape=out_shape,
        compiler_params=params(WHOLE),
        cost_estimate=cost(
            2 * CORES * Y * BLOCK * owners * depth * half, owners * 4 * 2**20
        ),
        name="serve",
    )(at, *args)
    return result if last else result[0]


def mix_kernel(keep_ref, peer_ref, own_ref, *refs):
    arrived, out_ref = refs[:-1], refs[-1]
    half = own_ref.shape[2]
    for core, ref in enumerate((keep_ref, peer_ref)):
        value = ref[:, :half] + own_ref[core]
        for part in arrived:
            value = value + part[core].astype(F32)
        scale = ref[:, half : half + 1]
        out_ref[core] = (scale * value).astype(BF16)


def mix(keep, peer, own, arrived):
    return pl.pallas_call(
        mix_kernel,
        out_shape=jax.ShapeDtypeStruct(own.shape, BF16),
        in_specs=[VMEM] * (3 + len(arrived)),
        out_specs=VMEM,
        compiler_params=params(),
        cost_estimate=cost(2**20, 2 * 2**20),
        name="mix",
    )(keep, peer, own, *arrived)


def halves(at_ref, ref):
    core = at_ref[1]
    half = ref.shape[0] // CORES
    mine = ref[pl.ds(pl.multiple_of(core * half, BLOCK), half), :]
    other = ref[pl.ds(pl.multiple_of((1 - core) * half, BLOCK), half), :]
    return mine, other


def row_pair(mine_ref, other_ref):
    shape = (CORES * BLOCK, mine_ref.shape[2])
    mine = mine_ref[...].reshape(shape)
    other = jnp.concatenate([other_ref[1], other_ref[0]], axis=0)
    return mine, other


def term_kernel(at_ref, weight_ref, grads_ref, *refs):
    mixed, outs, whole_ref = refs[: 2 * X], refs[2 * X : -1], refs[-1]
    core = at_ref[1]
    weight_mine, weight_other = halves(at_ref, weight_ref)
    half = weight_mine.shape[0]
    sums = [None, None]
    for step in range(X):
        rows = row_pair(mixed[2 * step], mixed[2 * step + 1])
        pre = jnp.dot(rows[0], weight_mine, preferred_element_type=F32) + jnp.dot(
            rows[1], weight_other, preferred_element_type=F32
        )
        grads = jnp.concatenate(
            [grads_ref[at_ref[2 + 2 * step + part]] for part in range(CORES)], axis=0
        )
        gated = (grads.astype(F32) * slope(pre)).T.astype(BF16)
        for part in range(CORES):
            product = jnp.dot(gated, rows[part], preferred_element_type=F32)
            sums[part] = product if sums[part] is None else sums[part] + product
    height = half // (Z * Y // CORES)
    whole_ref[pl.ds(pl.multiple_of(core * half, BLOCK), half), :] = sums[0].T
    whole_ref[pl.ds(pl.multiple_of((1 - core) * half, BLOCK), half), :] = sums[1].T
    for step, out_ref in enumerate(outs):
        column = lax.rem(at_ref[0] - step + Y, Y)
        for z in range(Z):
            start = pl.multiple_of((z * Y + column) * height, height)
            out_ref[z * height : (z + 1) * height, :] = whole_ref[pl.ds(start, height), :]


def weight_term(at, weight, grads, mixed):
    return pl.pallas_call(
        term_kernel,
        out_shape=[jax.ShapeDtypeStruct((weight.shape[0] // Y, weight.shape[1]), F32)] * Y,
        in_specs=[SMEM] + [VMEM] * (2 + len(mixed)),
        out_specs=[VMEM] * Y,
        scratch_shapes=[pltpu.VMEM(weight.shape, F32)],
        compiler_params=params(),
        cost_estimate=cost(2**29, 3 * 2**20),
        name="term",
    )(at, weight, grads, *mixed)


def fresh_kernel(at_ref, weight_ref, *refs):
    mixed, out_ref = refs[:-1], refs[-1]
    weight_mine, weight_other = halves(at_ref, weight_ref)
    for step in range(X):
        rows = row_pair(mixed[2 * step], mixed[2 * step + 1])
        pre = jnp.dot(rows[0], weight_mine, preferred_element_type=F32) + jnp.dot(
            rows[1], weight_other, preferred_element_type=F32
        )
        value = (pre / (1.0 + jnp.exp(-pre))).astype(BF16)
        for part in range(CORES):
            place = at_ref[2 + X * CORES + 2 * step + part]
            out_ref[place] = value[part * BLOCK : (part + 1) * BLOCK]


def fresh_blocks(at, weight, mixed):
    width = weight.shape[0]
    return pl.pallas_call(
        fresh_kernel,
        out_shape=jax.ShapeDtypeStruct((X * CORES, BLOCK, width), BF16),
        in_specs=[SMEM] + [VMEM] * (1 + len(mixed)),
        out_specs=VMEM,
        compiler_params=params(),
        cost_estimate=cost(2**31, 6 * 2**20),
        name="fresh",
    )(at, weight, *mixed)


def back_kernel(at_ref, weight_ref, mine_ref, other_ref, grad_ref, scale_ref, local_ref, out_ref):
    weight_mine, weight_other = halves(at_ref, weight_ref)
    pre = jnp.dot(mine_ref[0], weight_mine, preferred_element_type=F32) + jnp.dot(
        other_ref[1], weight_other, preferred_element_type=F32
    )
    gated = (grad_ref[...].astype(F32) * slope(pre)).astype(BF16)
    back = scale_ref[:, :1] * lax.dot_general(
        gated, weight_ref[...], (((1,), (1,)), ((), ())), preferred_element_type=F32
    )
    local = local_ref[...].astype(F32).T.astype(BF16)
    value, rest = back, back
    for _ in range(3):
        part = rest.astype(BF16)
        value = value + jnp.dot(local, part, preferred_element_type=F32)
        rest = rest - part.astype(F32)
    out_ref[...] = value.astype(BF16)


def input_rows(at, weight, mine, other, grad_fresh, scale, local):
    return pl.pallas_call(
        back_kernel,
        out_shape=jax.ShapeDtypeStruct(grad_fresh.shape, BF16),
        in_specs=[SMEM] + [VMEM] * 6,
        out_specs=VMEM,
        compiler_params=params(),
        cost_estimate=cost(2**29 + 2**28, 4 * 2**20),
        name="back",
    )(at, weight, mine, other, grad_fresh, scale, local)


def shards(
    history_in,
    batch_emb,
    weight,
    grad_fresh,
    edge_weight,
    request_block,
    request_count,
    batch_block,
):
    owner = lax.axis_index("dom")
    replica = lax.axis_index("rep")
    z, y = owner // Y, owner % Y
    x, core = replica // CORES, replica % CORES
    blocks, block, width = history_in.shape
    rows = batch_emb.shape[0]
    half = width // CORES

    columns = [[line * Y + column for line in range(Z)] for column in range(Y)]

    odd = x % 2
    some = blocks // 2
    table = lax.dynamic_slice(history_in, (odd * some, 0, core * half), (some, block, half))
    table = table.reshape(some * block, half)
    up, down = [table, shift_z(table, 1)], [table, shift_z(table, -1)]

    offsets = jnp.array([0, X - 1, 1, 2], jnp.int32)
    places = ((x + offsets) % X)[:, None] * CORES + jnp.stack([core, 1 - core])[None, :]
    places = places.reshape(-1)
    targets = jnp.take(batch_block[0], places)
    at = jnp.concatenate([jnp.stack([y, core]), places, targets]).astype(jnp.int32)

    valid = jnp.arange(CAP, dtype=jnp.int32)[None, :] < request_count[0][:, None]
    code = jnp.where(valid, request_block[0], -1)
    code = jnp.repeat(code, block, axis=1)
    *near, keep, give, local, scale = pack(at, edge_weight, code, batch_emb)
    peer = swap_core(give)

    full_weight = lax.all_gather(weight, "rep", axis=1, tiled=True)
    grads = lax.all_to_all(grad_fresh, "rep", split_axis=1, concat_axis=0, tiled=True)
    grads = grads.reshape(X * CORES, rows, -1)

    here = [near[0]] + [shift_y(near[step], step) for step in range(1, Y)]
    up[1], down[1], _, peer = lax.optimization_barrier((up[1], down[1], near, peer))
    up.append(shift_z(up[1], 1))
    down.append(shift_z(down[1], -1))

    def spread(one, other, *after):
        one, other, after = lax.optimization_barrier((one, other, after))
        return [swap_even(one), swap_odd(other)], after

    first, (here[1], here[3], full_weight, grads) = spread(
        up[1], down[1], here[1], here[3], full_weight, grads
    )
    up.append(shift_z(up[2], 1))
    down.append(shift_z(down[2], -1))
    stacked = jnp.stack(here)
    up[3], down[3], stacked, first = lax.optimization_barrier((up[3], down[3], stacked, first))
    second, (first,) = spread(up[2], down[2], first)
    up.append(shift_z(up[3], 1))
    there = swap_core(stacked)

    known = jnp.stack([y, odd * some, (1 - odd) * some, core])

    def served(steps, tables, total=None, **more):
        owners = jnp.stack([(z + step) % Z for step in steps])
        scalars = jnp.concatenate([known, owners]).astype(jnp.int32)
        return serve(scalars, here, there, tables, half, blocks * block, total, **more)

    total = served(
        (0, 7, 1), [[history_in], [up[1], first[0]], [down[1], first[1]]], own=True
    )
    middle = some * block // 2
    third, (second, total, last) = spread(up[3], down[3], second, total, up[4])
    fourth = [swap_even(last[:middle]), swap_odd(last[middle:])]
    total = served((6, 2), [[up[2], second[0]], [down[2], second[1]]], total)
    total = served((5, 3), [[up[3], third[0]], [down[3], third[1]]], total)
    sums = served((4,), [[up[4], *fourth]], total, last=True)

    arrived = [shift_y(sums[step], -step) for step in range(1, Y)]
    mixed = [mix(keep, peer, sums[0], arrived)]
    mixed += [shift_x(mixed[0], 1), shift_x(mixed[0], -1), shift_x(mixed[0], 2)]
    own_other = swap_core(mixed[0])
    input_grad = input_rows(at, full_weight, mixed[0], own_other, grad_fresh, scale, local)
    mixed[3], input_grad = lax.optimization_barrier((mixed[3], input_grad))
    mixed = [mixed[0], own_other] + [
        part for mine in mixed[1:] for part in (mine, swap_core(mine))
    ]
    terms = weight_term(at, weight, grads, mixed)
    others = [shift_y(terms[step], -step) for step in range(1, Y)]
    fresh_history = fresh_blocks(at, full_weight, mixed)
    others, fresh_history = lax.optimization_barrier((others, fresh_history))
    part = terms[0] + others[0] + others[1] + others[2]
    part = lax.all_to_all(
        part, "dom", split_axis=0, concat_axis=0, tiled=True, axis_index_groups=columns
    )
    total_rows = rows * Z * Y * X * CORES
    weight_grad = jnp.sum(part.reshape(Z, -1, weight.shape[1]), axis=0) / math.sqrt(total_rows)
    return (fresh_history, weight_grad, input_grad)


def solution(mesh):
    placed = (
        P("dom", None, None),
        P(("dom", "rep"), None),
        P(None, "rep"),
        P(("dom", "rep"), None),
        P(("dom", "rep"), None),
        P(("dom", "rep"), None, None),
        P(("dom", "rep"), None),
        P("dom", None),
    )
    return jax.shard_map(
        shards,
        mesh=mesh,
        in_specs=placed,
        out_specs=(P("dom", None, None), P("dom", "rep"), P(("dom", "rep"), None)),
        check_vma=False,
    )
```

```python
import functools
import math

import jax
import jax.numpy as jnp
from jax import lax
from jax.experimental import pallas as pl
from jax.experimental.pallas import tpu as pltpu
from jax.sharding import PartitionSpec as P

Z, Y, X, CORES = 8, 4, 4, 2
CAP = 2
KNOWN = 4
BLOCK = 128
NAMES = 16
BF16 = jnp.bfloat16
F32 = jnp.float32
VMEM = pl.BlockSpec(memory_space=pltpu.VMEM)
SMEM = pl.BlockSpec(memory_space=pltpu.SMEM)
LIMIT = 48 * 2**20
WHOLE = 60 * 2**20


def shift_z(value, step):
    pairs = [(z * Y + y, (z + step) % Z * Y + y) for z in range(Z) for y in range(Y)]
    return lax.ppermute(value, "dom", pairs)


def shift_y(value, step):
    pairs = [(z * Y + y, z * Y + (y + step) % Y) for z in range(Z) for y in range(Y)]
    return lax.ppermute(value, "dom", pairs)


def shift_x(value, step):
    pairs = [(x * CORES + c, (x + step) % X * CORES + c) for x in range(X) for c in range(CORES)]
    return lax.ppermute(value, "rep", pairs)


def swap_even(value):
    pairs = [(x * CORES + c, (x ^ 1) * CORES + c) for x in range(X) for c in range(CORES)]
    return lax.ppermute(value, "rep", pairs)


def swap_odd(value):
    pairs = [
        (x * CORES + c, (x - 1 + 2 * (x % 2)) % X * CORES + c) for x in range(X) for c in range(CORES)
    ]
    return lax.ppermute(value, "rep", pairs)


def swap_core(value):
    pairs = [(x * CORES + c, x * CORES + 1 - c) for x in range(X) for c in range(CORES)]
    return lax.ppermute(value, "rep", pairs)


def slope(value):
    sigma = 1.0 / (1.0 + jnp.exp(-value))
    return sigma * (1.0 + value * (1.0 - sigma))


def params(limit=LIMIT):
    return pltpu.CompilerParams(vmem_limit_bytes=limit)


def cost(flops, moved):
    return pl.CostEstimate(flops=flops, bytes_accessed=moved, transcendentals=0)


def pack_kernel(at_ref, edge_ref, code_ref, batch_ref, *outs):
    near, (keep_ref, give_ref, local_ref, scale_ref) = outs[:Y], outs[Y:]
    y, core = at_ref[0], at_ref[1]
    rows, width = batch_ref.shape
    half = width // CORES
    pair = CAP * BLOCK
    sums = jnp.zeros((rows, pair), jnp.int32)
    for step in range(Y):
        column = lax.rem(y + step, Y)
        for z in range(Z):
            slot = z * Y + column
            edges = edge_ref[:, pl.ds(pl.multiple_of(rows + slot * pair, BLOCK), pair)]
            code = code_ref[pl.ds(slot, 1), :]
            near[step][z, :rows, :] = edges.astype(F32).astype(BF16)
            near[step][z, rows:, :] = jnp.broadcast_to(code, (NAMES, pair)).astype(F32).astype(BF16)
            sums = sums + jnp.where(code >= 0, edges, 0)
    local = edge_ref[:, :rows].astype(F32)
    degree = (
        1.0
        + jnp.sum(local, axis=1, keepdims=True)
        + jnp.sum(sums.astype(F32), axis=1, keepdims=True)
    )
    scale = jnp.broadcast_to(lax.rsqrt(degree), (rows, BLOCK))
    scale_ref[...] = scale
    local_ref[...] = local.astype(BF16)
    for ref, part in ((keep_ref, core), (give_ref, 1 - core)):
        batch = batch_ref[:, pl.ds(pl.multiple_of(part * half, BLOCK), half)]
        ref[:, :half] = batch.astype(F32) + jnp.dot(
            local.astype(BF16), batch, preferred_element_type=F32
        )
        ref[:, half:] = scale


def pack(at, edge_weight, code, batch_emb):
    rows, width = batch_emb.shape
    half = width // CORES
    message = jax.ShapeDtypeStruct((Z, rows + NAMES, CAP * BLOCK), BF16)
    own = jax.ShapeDtypeStruct((rows, half + BLOCK), F32)
    return pl.pallas_call(
        pack_kernel,
        out_shape=[message] * Y
        + [
            own,
            own,
            jax.ShapeDtypeStruct((rows, rows), BF16),
            jax.ShapeDtypeStruct((rows, BLOCK), F32),
        ],
        in_specs=[SMEM, VMEM, VMEM, VMEM],
        out_specs=[VMEM] * (Y + 4),
        compiler_params=params(WHOLE),
        cost_estimate=cost(2 * rows * rows * width, 8 * 2**20),
        name="pack",
    )(at, edge_weight, code, batch_emb)


def serve_kernel(owners, parts, own, group, first, last, at_ref, *refs):
    each = Y + 1
    messages, refs = refs[: owners * each], refs[owners * each :]
    pieces, refs = refs[: sum(parts)], refs[sum(parts) :]
    if not first:
        total_ref, refs = refs[0], refs[1:]
    outs, (merged, tables) = refs[:-2], refs[-2:]
    depth = tables.shape[0] // owners

    @pl.when(pl.program_id(0) == 0)
    def _():
        row = 0
        for piece in pieces:
            value = piece[...].reshape(-1, piece.shape[-1])
            tables[row : row + value.shape[0], :] = value
            row += value.shape[0]

    for step in range(Y):

        @pl.when(pl.program_id(0) == step // group)
        def _(step=step):
            place_in = step % group
            top = place_in * CORES * BLOCK
            for owner in range(owners):
                for core in range(CORES):
                    ref = messages[owner * each + (Y if core else step)]
                    ref = ref.at[step, 0] if core else ref.at[0]
                    names = ref[BLOCK:, :].astype(F32)
                    body = ref[:BLOCK, :].reshape(BLOCK // NAMES, NAMES, CAP * BLOCK)
                    for place in range(depth // BLOCK):
                        block = float(place)
                        if not (own and owner == 0):
                            part, rest = divmod(place, depth // BLOCK // 2)
                            block = (at_ref[1 + part] + rest).astype(F32)
                        hit = jnp.where(names == block, 1.0, 0.0).astype(BF16)
                        part = body * hit[None]
                        both = part[:, :, :BLOCK] + part[:, :, BLOCK:]
                        column = owner * depth + place * BLOCK
                        row = top + core * BLOCK
                        merged[row : row + BLOCK, column : column + BLOCK] = both.reshape(
                            BLOCK, BLOCK
                        )
            value = jnp.dot(
                merged[top : top + CORES * BLOCK, :], tables[...], preferred_element_type=F32
            )
            value = value.reshape(CORES, BLOCK, value.shape[1])
            if not first:
                value = total_ref[:, place_in] + value
            if last:
                outs[step][...] = value.astype(outs[step].dtype)
            else:
                outs[0][:, place_in] = value


def serve(at, at_owners, here, there, tables, half, depth, total=None, last=False, own=False):
    owners = len(tables)
    group = Y if last else 2
    flat = [piece for pieces in tables for piece in pieces]

    def message_spec(owner):
        shape = (1,) + here[0].shape[1:]
        return pl.BlockSpec(shape, lambda i, at_ref: (at_ref[KNOWN + at_owners[owner]], 0, 0))

    def other_spec(owner):
        shape = (Y, 1) + here[0].shape[1:]
        return pl.BlockSpec(shape, lambda i, at_ref: (0, at_ref[KNOWN + at_owners[owner]], 0, 0))

    def piece_spec(piece):
        if piece.ndim == 3:
            shape = piece.shape[:2] + (half,)
            return pl.BlockSpec(shape, lambda i, at_ref: (0, 0, at_ref[KNOWN - 1]))
        return pl.BlockSpec(piece.shape, lambda i, at_ref: (0, 0))

    in_specs = []
    for owner in range(owners):
        in_specs += [message_spec(owner)] * Y + [other_spec(owner)]
    in_specs += [piece_spec(piece) for piece in flat]
    total_spec = pl.BlockSpec((CORES, group, BLOCK, half), lambda i, at_ref: (0, i, 0, 0))
    args = (list(here) + [there]) * owners + flat
    if total is not None:
        in_specs.append(total_spec)
        args.append(total)
    if last:
        out_shape = [
            jax.ShapeDtypeStruct((CORES, BLOCK, half), F32 if step == 0 else BF16)
            for step in range(Y)
        ]
        out_specs = [pl.BlockSpec((CORES, BLOCK, half), lambda i, at_ref: (0, 0, 0))] * Y
    else:
        out_shape = [jax.ShapeDtypeStruct((CORES, Y, BLOCK, half), F32)]
        out_specs = [total_spec]
    result = pl.pallas_call(
        functools.partial(
            serve_kernel,
            owners,
            [len(pieces) for pieces in tables],
            own,
            group,
            total is None,
            last,
        ),
        grid_spec=pltpu.PrefetchScalarGridSpec(
            num_scalar_prefetch=1,
            grid=(Y // group,),
            in_specs=in_specs,
            out_specs=out_specs,
            scratch_shapes=[
                pltpu.VMEM((group * CORES * BLOCK, owners * depth), BF16),
                pltpu.VMEM((owners * depth, half), BF16),
            ],
        ),
        out_shape=out_shape,
        compiler_params=params(WHOLE),
        cost_estimate=cost(
            2 * CORES * Y * BLOCK * owners * depth * half, owners * 4 * 2**20
        ),
        name="serve",
    )(at, *args)
    return result if last else result[0]


def mix_kernel(keep_ref, peer_ref, own_ref, *refs):
    arrived, out_ref = refs[:-1], refs[-1]
    half = own_ref.shape[2]
    for core, ref in enumerate((keep_ref, peer_ref)):
        value = ref[:, :half] + own_ref[core]
        for part in arrived:
            value = value + part[core].astype(F32)
        scale = ref[:, half : half + 1]
        out_ref[core] = (scale * value).astype(BF16)


def mix(keep, peer, own, arrived):
    return pl.pallas_call(
        mix_kernel,
        out_shape=jax.ShapeDtypeStruct(own.shape, BF16),
        in_specs=[VMEM] * (3 + len(arrived)),
        out_specs=VMEM,
        compiler_params=params(),
        cost_estimate=cost(2**20, 2 * 2**20),
        name="mix",
    )(keep, peer, own, *arrived)


def halves(at_ref, ref):
    core = at_ref[1]
    half = ref.shape[0] // CORES
    mine = ref[pl.ds(pl.multiple_of(core * half, BLOCK), half), :]
    other = ref[pl.ds(pl.multiple_of((1 - core) * half, BLOCK), half), :]
    return mine, other


def row_pair(mine_ref, other_ref):
    shape = (CORES * BLOCK, mine_ref.shape[2])
    mine = mine_ref[...].reshape(shape)
    other = jnp.concatenate([other_ref[1], other_ref[0]], axis=0)
    return mine, other


def term_kernel(at_ref, weight_ref, grads_ref, *refs):
    mixed, outs, whole_ref = refs[: 2 * X], refs[2 * X : -1], refs[-1]
    core = at_ref[1]
    weight_mine, weight_other = halves(at_ref, weight_ref)
    half = weight_mine.shape[0]
    sums = [None, None]
    for step in range(X):
        rows = row_pair(mixed[2 * step], mixed[2 * step + 1])
        pre = jnp.dot(rows[0], weight_mine, preferred_element_type=F32) + jnp.dot(
            rows[1], weight_other, preferred_element_type=F32
        )
        grads = jnp.concatenate(
            [grads_ref[at_ref[2 + 2 * step + part]] for part in range(CORES)], axis=0
        )
        gated = (grads.astype(F32) * slope(pre)).T.astype(BF16)
        for part in range(CORES):
            product = jnp.dot(gated, rows[part], preferred_element_type=F32)
            sums[part] = product if sums[part] is None else sums[part] + product
    height = half // (Z * Y // CORES)
    whole_ref[pl.ds(pl.multiple_of(core * half, BLOCK), half), :] = sums[0].T
    whole_ref[pl.ds(pl.multiple_of((1 - core) * half, BLOCK), half), :] = sums[1].T
    for step, out_ref in enumerate(outs):
        column = lax.rem(at_ref[0] - step + Y, Y)
        for z in range(Z):
            start = pl.multiple_of((z * Y + column) * height, height)
            out_ref[z * height : (z + 1) * height, :] = whole_ref[pl.ds(start, height), :]


def weight_term(at, weight, grads, mixed):
    return pl.pallas_call(
        term_kernel,
        out_shape=[jax.ShapeDtypeStruct((weight.shape[0] // Y, weight.shape[1]), F32)] * Y,
        in_specs=[SMEM] + [VMEM] * (2 + len(mixed)),
        out_specs=[VMEM] * Y,
        scratch_shapes=[pltpu.VMEM(weight.shape, F32)],
        compiler_params=params(),
        cost_estimate=cost(2**29, 3 * 2**20),
        name="term",
    )(at, weight, grads, *mixed)


def fresh_kernel(at_ref, weight_ref, *refs):
    mixed, out_ref = refs[:-1], refs[-1]
    weight_mine, weight_other = halves(at_ref, weight_ref)
    for step in range(X):
        rows = row_pair(mixed[2 * step], mixed[2 * step + 1])
        pre = jnp.dot(rows[0], weight_mine, preferred_element_type=F32) + jnp.dot(
            rows[1], weight_other, preferred_element_type=F32
        )
        value = (pre / (1.0 + jnp.exp(-pre))).astype(BF16)
        for part in range(CORES):
            place = at_ref[2 + X * CORES + 2 * step + part]
            out_ref[place] = value[part * BLOCK : (part + 1) * BLOCK]


def fresh_blocks(at, weight, mixed):
    width = weight.shape[0]
    return pl.pallas_call(
        fresh_kernel,
        out_shape=jax.ShapeDtypeStruct((X * CORES, BLOCK, width), BF16),
        in_specs=[SMEM] + [VMEM] * (1 + len(mixed)),
        out_specs=VMEM,
        compiler_params=params(),
        cost_estimate=cost(2**31, 6 * 2**20),
        name="fresh",
    )(at, weight, *mixed)


def back_kernel(at_ref, weight_ref, mine_ref, other_ref, grad_ref, scale_ref, local_ref, out_ref):
    weight_mine, weight_other = halves(at_ref, weight_ref)
    pre = jnp.dot(mine_ref[0], weight_mine, preferred_element_type=F32) + jnp.dot(
        other_ref[1], weight_other, preferred_element_type=F32
    )
    gated = (grad_ref[...].astype(F32) * slope(pre)).astype(BF16)
    back = scale_ref[:, :1] * lax.dot_general(
        gated, weight_ref[...], (((1,), (1,)), ((), ())), preferred_element_type=F32
    )
    local = local_ref[...].astype(F32).T.astype(BF16)
    value, rest = back, back
    for _ in range(3):
        part = rest.astype(BF16)
        value = value + jnp.dot(local, part, preferred_element_type=F32)
        rest = rest - part.astype(F32)
    out_ref[...] = value.astype(BF16)


def input_rows(at, weight, mine, other, grad_fresh, scale, local):
    return pl.pallas_call(
        back_kernel,
        out_shape=jax.ShapeDtypeStruct(grad_fresh.shape, BF16),
        in_specs=[SMEM] + [VMEM] * 6,
        out_specs=VMEM,
        compiler_params=params(),
        cost_estimate=cost(2**29 + 2**28, 4 * 2**20),
        name="back",
    )(at, weight, mine, other, grad_fresh, scale, local)


def shards(
    history_in,
    batch_emb,
    weight,
    grad_fresh,
    edge_weight,
    request_block,
    request_count,
    batch_block,
):
    owner = lax.axis_index("dom")
    replica = lax.axis_index("rep")
    z, y = owner // Y, owner % Y
    x, core = replica // CORES, replica % CORES
    blocks, block, width = history_in.shape
    rows = batch_emb.shape[0]
    half = width // CORES

    columns = [[line * Y + column for line in range(Z)] for column in range(Y)]

    odd = x % 2
    some = blocks // 2
    table = lax.dynamic_slice(history_in, (odd * some, 0, core * half), (some, block, half))
    table = table.reshape(some * block, half)
    up, down = [table, shift_z(table, 1)], [table, shift_z(table, -1)]

    offsets = jnp.array([0, X - 1, 1, 2], jnp.int32)
    places = ((x + offsets) % X)[:, None] * CORES + jnp.stack([core, 1 - core])[None, :]
    places = places.reshape(-1)
    targets = jnp.take(batch_block[0], places)
    at = jnp.concatenate([jnp.stack([y, core]), places, targets]).astype(jnp.int32)

    valid = jnp.arange(CAP, dtype=jnp.int32)[None, :] < request_count[0][:, None]
    code = jnp.where(valid, request_block[0], -1)
    code = jnp.repeat(code, block, axis=1)
    *near, keep, give, local, scale = pack(at, edge_weight, code, batch_emb)
    peer = swap_core(give)

    full_weight = lax.all_gather(weight, "rep", axis=1, tiled=True)
    here = [near[0]] + [shift_y(near[step], step) for step in range(1, Y)]
    up[1], down[1], _, peer = lax.optimization_barrier((up[1], down[1], near, peer))
    up.append(shift_z(up[1], 1))
    down.append(shift_z(down[1], -1))

    def spread(one, other, *after):
        one, other, after = lax.optimization_barrier((one, other, after))
        return [swap_even(one), swap_odd(other)], after

    first, (here[1], here[3], full_weight) = spread(
        up[1], down[1], here[1], here[3], full_weight
    )
    up[2], down[2], late = lax.optimization_barrier((up[2], down[2], grad_fresh))
    grads = lax.all_to_all(late, "rep", split_axis=1, concat_axis=0, tiled=True)
    grads = grads.reshape(X * CORES, rows, -1)
    up.append(shift_z(up[2], 1))
    down.append(shift_z(down[2], -1))
    second, (here[2],) = spread(up[2], down[2], here[2])
    stacked = jnp.stack(here)
    up[3], down[3], stacked, first, grads = lax.optimization_barrier(
        (up[3], down[3], stacked, first, grads)
    )
    third, _ = spread(up[3], down[3])
    up.append(shift_z(up[3], 1))
    there = swap_core(stacked)

    known = jnp.stack(
        [y, odd * some, (1 - odd) * some, core] + [(z + step) % Z for step in range(Z)]
    ).astype(jnp.int32)

    def served(steps, tables, total=None, **more):
        return serve(known, steps, here, there, tables, half, blocks * block, total, **more)

    total = served(
        (0, 7, 1), [[history_in], [up[1], first[0]], [down[1], first[1]]], own=True
    )
    middle = some * block // 2
    last, second, total = lax.optimization_barrier((up[4], second, total))
    fourth = [swap_even(last[:middle]), swap_odd(last[middle:])]
    total = served((6, 2), [[up[2], second[0]], [down[2], second[1]]], total)
    total = served((5, 3), [[up[3], third[0]], [down[3], third[1]]], total)
    sums = served((4,), [[up[4], *fourth]], total, last=True)

    arrived = [shift_y(sums[step], -step) for step in range(1, Y)]
    mixed = [mix(keep, peer, sums[0], arrived)]
    mixed += [shift_x(mixed[0], 1), shift_x(mixed[0], -1), shift_x(mixed[0], 2)]
    own_other = swap_core(mixed[0])
    input_grad = input_rows(at, full_weight, mixed[0], own_other, grad_fresh, scale, local)
    mixed[3], input_grad = lax.optimization_barrier((mixed[3], input_grad))
    mixed = [mixed[0], own_other] + [
        part for mine in mixed[1:] for part in (mine, swap_core(mine))
    ]
    terms = weight_term(at, weight, grads, mixed)
    others = [shift_y(terms[step], -step) for step in range(1, Y)]
    fresh_history = fresh_blocks(at, full_weight, mixed)
    others, fresh_history = lax.optimization_barrier((others, fresh_history))
    part = terms[0] + others[0] + others[1] + others[2]
    part = lax.all_to_all(
        part, "dom", split_axis=0, concat_axis=0, tiled=True, axis_index_groups=columns
    )
    total_rows = rows * Z * Y * X * CORES
    weight_grad = jnp.sum(part.reshape(Z, -1, weight.shape[1]), axis=0) / math.sqrt(total_rows)
    return (fresh_history, weight_grad, input_grad)


def solution(mesh):
    placed = (
        P("dom", None, None),
        P(("dom", "rep"), None),
        P(None, "rep"),
        P(("dom", "rep"), None),
        P(("dom", "rep"), None),
        P(("dom", "rep"), None, None),
        P(("dom", "rep"), None),
        P("dom", None),
    )
    return jax.shard_map(
        shards,
        mesh=mesh,
        in_specs=placed,
        out_specs=(P("dom", None, None), P("dom", "rep"), P(("dom", "rep"), None)),
        check_vma=False,
    )
```

```python
import functools
import math

import jax
import jax.numpy as jnp
from jax import lax
from jax.experimental import pallas as pl
from jax.experimental.pallas import tpu as pltpu
from jax.sharding import PartitionSpec as P

Z, Y, X, CORES = 8, 4, 4, 2
CAP = 2
KNOWN = 4
BLOCK = 128
NAMES = 16
BF16 = jnp.bfloat16
F32 = jnp.float32
VMEM = pl.BlockSpec(memory_space=pltpu.VMEM)
SMEM = pl.BlockSpec(memory_space=pltpu.SMEM)
LIMIT = 48 * 2**20
WHOLE = 60 * 2**20


def shift_z(value, step):
    pairs = [(z * Y + y, (z + step) % Z * Y + y) for z in range(Z) for y in range(Y)]
    return lax.ppermute(value, "dom", pairs)


def shift_y(value, step):
    pairs = [(z * Y + y, z * Y + (y + step) % Y) for z in range(Z) for y in range(Y)]
    return lax.ppermute(value, "dom", pairs)


def shift_x(value, step):
    pairs = [(x * CORES + c, (x + step) % X * CORES + c) for x in range(X) for c in range(CORES)]
    return lax.ppermute(value, "rep", pairs)


def swap_even(value):
    pairs = [(x * CORES + c, (x ^ 1) * CORES + c) for x in range(X) for c in range(CORES)]
    return lax.ppermute(value, "rep", pairs)


def swap_odd(value):
    pairs = [
        (x * CORES + c, (x - 1 + 2 * (x % 2)) % X * CORES + c) for x in range(X) for c in range(CORES)
    ]
    return lax.ppermute(value, "rep", pairs)


def swap_core(value):
    pairs = [(x * CORES + c, x * CORES + 1 - c) for x in range(X) for c in range(CORES)]
    return lax.ppermute(value, "rep", pairs)


def slope(value):
    sigma = 1.0 / (1.0 + jnp.exp(-value))
    return sigma * (1.0 + value * (1.0 - sigma))


def params(limit=LIMIT):
    return pltpu.CompilerParams(vmem_limit_bytes=limit)


def cost(flops, moved):
    return pl.CostEstimate(flops=flops, bytes_accessed=moved, transcendentals=0)


def pack_kernel(at_ref, edge_ref, code_ref, batch_ref, *outs):
    near, (keep_ref, give_ref, local_ref, scale_ref) = outs[:Y], outs[Y:]
    y, core = at_ref[0], at_ref[1]
    rows, width = batch_ref.shape
    half = width // CORES
    pair = CAP * BLOCK
    sums = jnp.zeros((rows, pair), jnp.int32)
    for step in range(Y):
        column = lax.rem(y + step, Y)
        for z in range(Z):
            slot = z * Y + column
            edges = edge_ref[:, pl.ds(pl.multiple_of(rows + slot * pair, BLOCK), pair)]
            code = code_ref[pl.ds(slot, 1), :]
            near[step][z, :rows, :] = edges.astype(F32).astype(BF16)
            near[step][z, rows:, :] = jnp.broadcast_to(code, (NAMES, pair)).astype(F32).astype(BF16)
            sums = sums + jnp.where(code >= 0, edges, 0)
    local = edge_ref[:, :rows].astype(F32)
    degree = (
        1.0
        + jnp.sum(local, axis=1, keepdims=True)
        + jnp.sum(sums.astype(F32), axis=1, keepdims=True)
    )
    scale = jnp.broadcast_to(lax.rsqrt(degree), (rows, BLOCK))
    scale_ref[...] = scale
    local_ref[...] = local.astype(BF16)
    for ref, part in ((keep_ref, core), (give_ref, 1 - core)):
        batch = batch_ref[:, pl.ds(pl.multiple_of(part * half, BLOCK), half)]
        ref[:, :half] = batch.astype(F32) + jnp.dot(
            local.astype(BF16), batch, preferred_element_type=F32
        )
        ref[:, half:] = scale


def pack(at, edge_weight, code, batch_emb):
    rows, width = batch_emb.shape
    half = width // CORES
    message = jax.ShapeDtypeStruct((Z, rows + NAMES, CAP * BLOCK), BF16)
    own = jax.ShapeDtypeStruct((rows, half + BLOCK), F32)
    return pl.pallas_call(
        pack_kernel,
        out_shape=[message] * Y
        + [
            own,
            own,
            jax.ShapeDtypeStruct((rows, rows), BF16),
            jax.ShapeDtypeStruct((rows, BLOCK), F32),
        ],
        in_specs=[SMEM, VMEM, VMEM, VMEM],
        out_specs=[VMEM] * (Y + 4),
        compiler_params=params(WHOLE),
        cost_estimate=cost(2 * rows * rows * width, 8 * 2**20),
        name="pack",
    )(at, edge_weight, code, batch_emb)


def serve_kernel(owners, parts, own, group, first, last, at_ref, *refs):
    messages, refs = refs[: owners * CORES], refs[owners * CORES :]
    pieces, refs = refs[: sum(parts)], refs[sum(parts) :]
    if not first:
        total_ref, refs = refs[0], refs[1:]
    outs, (merged, tables) = refs[:-2], refs[-2:]
    depth = tables.shape[0] // owners

    @pl.when(pl.program_id(0) == 0)
    def _():
        row = 0
        for piece in pieces:
            value = piece[...].reshape(-1, piece.shape[-1])
            tables[row : row + value.shape[0], :] = value
            row += value.shape[0]

    for step in range(group):
        top = step * CORES * BLOCK
        for owner in range(owners):
            for core in range(CORES):
                ref = messages[owner * CORES + core].at[step, 0]
                names = ref[BLOCK:, :].astype(F32)
                body = ref[:BLOCK, :].reshape(BLOCK // NAMES, NAMES, CAP * BLOCK)
                for place in range(depth // BLOCK):
                    block = float(place)
                    if not (own and owner == 0):
                        part, rest = divmod(place, depth // BLOCK // 2)
                        block = (at_ref[1 + part] + rest).astype(F32)
                    hit = jnp.where(names == block, 1.0, 0.0).astype(BF16)
                    part = body * hit[None]
                    both = part[:, :, :BLOCK] + part[:, :, BLOCK:]
                    column = owner * depth + place * BLOCK
                    row = top + core * BLOCK
                    merged[row : row + BLOCK, column : column + BLOCK] = both.reshape(
                        BLOCK, BLOCK
                    )
        value = jnp.dot(
            merged[top : top + CORES * BLOCK, :], tables[...], preferred_element_type=F32
        )
        value = value.reshape(CORES, BLOCK, value.shape[1])
        if not first:
            value = total_ref[:, step] + value
        if last:
            outs[step][...] = value.astype(outs[step].dtype)
        else:
            outs[0][:, step] = value


def serve(at, at_owners, here, there, tables, half, depth, total=None, last=False, own=False):
    owners = len(tables)
    group = Y if last else 1
    flat = [piece for pieces in tables for piece in pieces]

    def message_spec(owner):
        shape = (group, 1) + here.shape[2:]
        return pl.BlockSpec(shape, lambda i, at_ref: (i, at_ref[KNOWN + at_owners[owner]], 0, 0))

    def piece_spec(piece):
        if piece.ndim == 3:
            shape = piece.shape[:2] + (half,)
            return pl.BlockSpec(shape, lambda i, at_ref: (0, 0, at_ref[KNOWN - 1]))
        return pl.BlockSpec(piece.shape, lambda i, at_ref: (0, 0))

    in_specs = []
    for owner in range(owners):
        in_specs += [message_spec(owner)] * CORES
    in_specs += [piece_spec(piece) for piece in flat]
    total_spec = pl.BlockSpec((CORES, group, BLOCK, half), lambda i, at_ref: (0, i, 0, 0))
    args = [here, there] * owners + flat
    if total is not None:
        in_specs.append(total_spec)
        args.append(total)
    if last:
        out_shape = [
            jax.ShapeDtypeStruct((CORES, BLOCK, half), F32 if step == 0 else BF16)
            for step in range(Y)
        ]
        out_specs = [pl.BlockSpec((CORES, BLOCK, half), lambda i, at_ref: (0, 0, 0))] * Y
    else:
        out_shape = [jax.ShapeDtypeStruct((CORES, Y, BLOCK, half), F32)]
        out_specs = [total_spec]
    result = pl.pallas_call(
        functools.partial(
            serve_kernel,
            owners,
            [len(pieces) for pieces in tables],
            own,
            group,
            total is None,
            last,
        ),
        grid_spec=pltpu.PrefetchScalarGridSpec(
            num_scalar_prefetch=1,
            grid=(Y // group,),
            in_specs=in_specs,
            out_specs=out_specs,
            scratch_shapes=[
                pltpu.VMEM((group * CORES * BLOCK, owners * depth), BF16),
                pltpu.VMEM((owners * depth, half), BF16),
            ],
        ),
        out_shape=out_shape,
        compiler_params=params(WHOLE),
        cost_estimate=cost(
            2 * CORES * Y * BLOCK * owners * depth * half, owners * 4 * 2**20
        ),
        name="serve",
    )(at, *args)
    return result if last else result[0]


def mix_kernel(keep_ref, peer_ref, own_ref, *refs):
    arrived, out_ref = refs[:-1], refs[-1]
    half = own_ref.shape[2]
    for core, ref in enumerate((keep_ref, peer_ref)):
        value = ref[:, :half] + own_ref[core]
        for part in arrived:
            value = value + part[core].astype(F32)
        scale = ref[:, half : half + 1]
        out_ref[core] = (scale * value).astype(BF16)


def mix(keep, peer, own, arrived):
    return pl.pallas_call(
        mix_kernel,
        out_shape=jax.ShapeDtypeStruct(own.shape, BF16),
        in_specs=[VMEM] * (3 + len(arrived)),
        out_specs=VMEM,
        compiler_params=params(),
        cost_estimate=cost(2**20, 2 * 2**20),
        name="mix",
    )(keep, peer, own, *arrived)


def halves(at_ref, ref):
    core = at_ref[1]
    half = ref.shape[0] // CORES
    mine = ref[pl.ds(pl.multiple_of(core * half, BLOCK), half), :]
    other = ref[pl.ds(pl.multiple_of((1 - core) * half, BLOCK), half), :]
    return mine, other


def row_pair(mine_ref, other_ref):
    shape = (CORES * BLOCK, mine_ref.shape[2])
    mine = mine_ref[...].reshape(shape)
    other = jnp.concatenate([other_ref[1], other_ref[0]], axis=0)
    return mine, other


def term_kernel(at_ref, weight_ref, grads_ref, *refs):
    mixed, outs, whole_ref = refs[: 2 * X], refs[2 * X : -1], refs[-1]
    core = at_ref[1]
    weight_mine, weight_other = halves(at_ref, weight_ref)
    half = weight_mine.shape[0]
    sums = [None, None]
    for step in range(X):
        rows = row_pair(mixed[2 * step], mixed[2 * step + 1])
        pre = jnp.dot(rows[0], weight_mine, preferred_element_type=F32) + jnp.dot(
            rows[1], weight_other, preferred_element_type=F32
        )
        grads = jnp.concatenate(
            [grads_ref[at_ref[2 + 2 * step + part]] for part in range(CORES)], axis=0
        )
        gated = (grads.astype(F32) * slope(pre)).T.astype(BF16)
        for part in range(CORES):
            product = jnp.dot(gated, rows[part], preferred_element_type=F32)
            sums[part] = product if sums[part] is None else sums[part] + product
    height = half // (Z * Y // CORES)
    whole_ref[pl.ds(pl.multiple_of(core * half, BLOCK), half), :] = sums[0].T
    whole_ref[pl.ds(pl.multiple_of((1 - core) * half, BLOCK), half), :] = sums[1].T
    for step, out_ref in enumerate(outs):
        column = lax.rem(at_ref[0] - step + Y, Y)
        for z in range(Z):
            start = pl.multiple_of((z * Y + column) * height, height)
            out_ref[z * height : (z + 1) * height, :] = whole_ref[pl.ds(start, height), :]


def weight_term(at, weight, grads, mixed):
    return pl.pallas_call(
        term_kernel,
        out_shape=[jax.ShapeDtypeStruct((weight.shape[0] // Y, weight.shape[1]), F32)] * Y,
        in_specs=[SMEM] + [VMEM] * (2 + len(mixed)),
        out_specs=[VMEM] * Y,
        scratch_shapes=[pltpu.VMEM(weight.shape, F32)],
        compiler_params=params(),
        cost_estimate=cost(2**29, 3 * 2**20),
        name="term",
    )(at, weight, grads, *mixed)


def fresh_kernel(at_ref, weight_ref, *refs):
    mixed, out_ref = refs[:-1], refs[-1]
    weight_mine, weight_other = halves(at_ref, weight_ref)
    for step in range(X):
        rows = row_pair(mixed[2 * step], mixed[2 * step + 1])
        pre = jnp.dot(rows[0], weight_mine, preferred_element_type=F32) + jnp.dot(
            rows[1], weight_other, preferred_element_type=F32
        )
        value = (pre / (1.0 + jnp.exp(-pre))).astype(BF16)
        for part in range(CORES):
            place = at_ref[2 + X * CORES + 2 * step + part]
            out_ref[place] = value[part * BLOCK : (part + 1) * BLOCK]


def fresh_blocks(at, weight, mixed):
    width = weight.shape[0]
    return pl.pallas_call(
        fresh_kernel,
        out_shape=jax.ShapeDtypeStruct((X * CORES, BLOCK, width), BF16),
        in_specs=[SMEM] + [VMEM] * (1 + len(mixed)),
        out_specs=VMEM,
        compiler_params=params(),
        cost_estimate=cost(2**31, 6 * 2**20),
        name="fresh",
    )(at, weight, *mixed)


def back_kernel(at_ref, weight_ref, mine_ref, other_ref, grad_ref, scale_ref, local_ref, out_ref):
    weight_mine, weight_other = halves(at_ref, weight_ref)
    pre = jnp.dot(mine_ref[0], weight_mine, preferred_element_type=F32) + jnp.dot(
        other_ref[1], weight_other, preferred_element_type=F32
    )
    gated = (grad_ref[...].astype(F32) * slope(pre)).astype(BF16)
    back = scale_ref[:, :1] * lax.dot_general(
        gated, weight_ref[...], (((1,), (1,)), ((), ())), preferred_element_type=F32
    )
    local = local_ref[...].astype(F32).T.astype(BF16)
    value, rest = back, back
    for _ in range(3):
        part = rest.astype(BF16)
        value = value + jnp.dot(local, part, preferred_element_type=F32)
        rest = rest - part.astype(F32)
    out_ref[...] = value.astype(BF16)


def input_rows(at, weight, mine, other, grad_fresh, scale, local):
    return pl.pallas_call(
        back_kernel,
        out_shape=jax.ShapeDtypeStruct(grad_fresh.shape, BF16),
        in_specs=[SMEM] + [VMEM] * 6,
        out_specs=VMEM,
        compiler_params=params(),
        cost_estimate=cost(2**29 + 2**28, 4 * 2**20),
        name="back",
    )(at, weight, mine, other, grad_fresh, scale, local)


def shards(
    history_in,
    batch_emb,
    weight,
    grad_fresh,
    edge_weight,
    request_block,
    request_count,
    batch_block,
):
    owner = lax.axis_index("dom")
    replica = lax.axis_index("rep")
    z, y = owner // Y, owner % Y
    x, core = replica // CORES, replica % CORES
    blocks, block, width = history_in.shape
    rows = batch_emb.shape[0]
    half = width // CORES

    columns = [[line * Y + column for line in range(Z)] for column in range(Y)]

    odd = x % 2
    some = blocks // 2
    table = lax.dynamic_slice(history_in, (odd * some, 0, core * half), (some, block, half))
    table = table.reshape(some * block, half)
    up, down = [table, shift_z(table, 1)], [table, shift_z(table, -1)]

    offsets = jnp.array([0, X - 1, 1, 2], jnp.int32)
    places = ((x + offsets) % X)[:, None] * CORES + jnp.stack([core, 1 - core])[None, :]
    places = places.reshape(-1)
    targets = jnp.take(batch_block[0], places)
    at = jnp.concatenate([jnp.stack([y, core]), places, targets]).astype(jnp.int32)

    valid = jnp.arange(CAP, dtype=jnp.int32)[None, :] < request_count[0][:, None]
    code = jnp.where(valid, request_block[0], -1)
    code = jnp.repeat(code, block, axis=1)
    *near, keep, give, local, scale = pack(at, edge_weight, code, batch_emb)
    peer = swap_core(give)

    full_weight = lax.all_gather(weight, "rep", axis=1, tiled=True)
    here = [near[0]] + [shift_y(near[step], step) for step in range(1, Y)]
    up[1], down[1], _, peer = lax.optimization_barrier((up[1], down[1], near, peer))
    up.append(shift_z(up[1], 1))
    down.append(shift_z(down[1], -1))

    def spread(one, other, *after):
        one, other, after = lax.optimization_barrier((one, other, after))
        return [swap_even(one), swap_odd(other)], after

    first, (here[1], here[3], full_weight) = spread(
        up[1], down[1], here[1], here[3], full_weight
    )
    up[2], down[2], late = lax.optimization_barrier((up[2], down[2], grad_fresh))
    grads = lax.all_to_all(late, "rep", split_axis=1, concat_axis=0, tiled=True)
    grads = grads.reshape(X * CORES, rows, -1)
    up.append(shift_z(up[2], 1))
    down.append(shift_z(down[2], -1))
    second, (here[2],) = spread(up[2], down[2], here[2])
    stacked = jnp.stack(here)
    up[3], down[3], stacked, first, grads = lax.optimization_barrier(
        (up[3], down[3], stacked, first, grads)
    )
    third, _ = spread(up[3], down[3])
    up.append(shift_z(up[3], 1))
    there = swap_core(stacked)

    known = jnp.stack(
        [y, odd * some, (1 - odd) * some, core] + [(z + step) % Z for step in range(Z)]
    ).astype(jnp.int32)

    def served(steps, tables, total=None, **more):
        return serve(known, steps, stacked, there, tables, half, blocks * block, total, **more)

    total = served(
        (0, 7, 1), [[history_in], [up[1], first[0]], [down[1], first[1]]], own=True
    )
    middle = some * block // 2
    last, second, total = lax.optimization_barrier((up[4], second, total))
    fourth = [swap_even(last[:middle]), swap_odd(last[middle:])]
    total = served((6, 2), [[up[2], second[0]], [down[2], second[1]]], total)
    total = served((5, 3), [[up[3], third[0]], [down[3], third[1]]], total)
    sums = served((4,), [[up[4], *fourth]], total, last=True)

    arrived = [shift_y(sums[step], -step) for step in range(1, Y)]
    mixed = [mix(keep, peer, sums[0], arrived)]
    mixed += [shift_x(mixed[0], 1), shift_x(mixed[0], -1), shift_x(mixed[0], 2)]
    own_other = swap_core(mixed[0])
    input_grad = input_rows(at, full_weight, mixed[0], own_other, grad_fresh, scale, local)
    mixed[3], input_grad = lax.optimization_barrier((mixed[3], input_grad))
    mixed = [mixed[0], own_other] + [
        part for mine in mixed[1:] for part in (mine, swap_core(mine))
    ]
    terms = weight_term(at, weight, grads, mixed)
    others = [shift_y(terms[step], -step) for step in range(1, Y)]
    fresh_history = fresh_blocks(at, full_weight, mixed)
    others, fresh_history = lax.optimization_barrier((others, fresh_history))
    part = terms[0] + others[0] + others[1] + others[2]
    part = lax.all_to_all(
        part, "dom", split_axis=0, concat_axis=0, tiled=True, axis_index_groups=columns
    )
    total_rows = rows * Z * Y * X * CORES
    weight_grad = jnp.sum(part.reshape(Z, -1, weight.shape[1]), axis=0) / math.sqrt(total_rows)
    return (fresh_history, weight_grad, input_grad)


def solution(mesh):
    placed = (
        P("dom", None, None),
        P(("dom", "rep"), None),
        P(None, "rep"),
        P(("dom", "rep"), None),
        P(("dom", "rep"), None),
        P(("dom", "rep"), None, None),
        P(("dom", "rep"), None),
        P("dom", None),
    )
    return jax.shard_map(
        shards,
        mesh=mesh,
        in_specs=placed,
        out_specs=(P("dom", None, None), P("dom", "rep"), P(("dom", "rep"), None)),
        check_vma=False,
    )
```
